256 devices in a mesh: section: 8 (over x, core), tensor: 8 (over z_hi, y), dp: 4 (over z_lo).
Axes of the slice: x: 4, y: 4, z: 8 (z_hi: 2, z_lo: 4; z = z_hi * 4 + z_lo), core: 2. Of those that a mesh axis runs over, the one named last changes fastest.
Arguments:
- handed_on: bfloat16 [8, 4, 128, 12288], P('section', 'dp', 'tensor'), may hold values from -6 to 6
- handed_back: bfloat16 [8, 4, 128, 12288], P('section', 'dp', 'tensor'), may hold values from -6 to 6
- fresh: bfloat16 [8, 4, 128, 48, 384], P('section', 'dp', None, 'tensor')
- evicted: bfloat16 [8, 4, 4, 128, 48, 384], P('section', None, 'dp', None, 'tensor')
- plan: int32 [8, 4], P('section', 'dp'), may hold values from 0 to 3
- w_out: bfloat16 [8, 6144, 12288], P('section', 'tensor', 'dp'), may hold values from -0.078125 to 0.078125
Outputs:
- layer_out: bfloat16 [8, 4, 128, 12288], P('section', 'dp', 'tensor')
- grad_qkv: bfloat16 [8, 4, 128, 48, 384], P('section', 'dp', None, 'tensor')
The draws below stay inside these ranges and needn't reach their ends.
All inputs are finite; a program needn't handle non-finite values.
Results may differ from the reference program's by a relative error of at most 0.02.
Values may be sent and summed in bfloat16 or wider, within the bound.
No kernel may reach another device: no remote copies, remote signals or barrier semaphores. Data moves between devices by JAX's collectives and lax.ppermute only.
A program may use at most 128 MiB of HBM per device.

```python
import math
import jax
import jax.numpy as jnp
from jax import lax

D = 12288
HEADS = 48
HD = 128
TOK = 128
SLOTS = 4
N_SECTION = 8
N_TENSOR = 8
N_DP = 4


def draw_fresh(key, part):
    key = jax.random.fold_in(key, 11)
    shape = (N_SECTION, N_DP, TOK, HEADS, 3 * HD)
    values = jax.random.truncated_normal(key, -4.0, 4.0, shape, jnp.float32)
    return values.astype(jnp.bfloat16)


def draw_evicted(key, part):
    key = jax.random.fold_in(key, 37)
    shape = (N_SECTION, SLOTS, N_DP, TOK, HEADS, 3 * HD)
    values = jax.random.truncated_normal(key, -4.0, 4.0, shape, jnp.float32)
    return values.astype(jnp.bfloat16)


def set_ends(values, key, low, largest):
    index_at = [jax.random.randint(jax.random.fold_in(key, axis), (), 0, length) for axis, length in enumerate(values.shape)]
    main_axis = values.shape.index(max(values.shape))
    next_to = index_at[:main_axis] + [(index_at[main_axis] + 1) % values.shape[main_axis]] + index_at[main_axis + 1:]
    return values.at[tuple(index_at)].set(low).at[tuple(next_to)].set(largest)


def block_levels(rng, shape, pieces, smallest, high):
    def one(dim, blocks):
        draws = jax.random.uniform(jax.random.fold_in(jax.random.fold_in(rng, 6), dim), (blocks,), jnp.float32, smallest / len(pieces), high / len(pieces))
        return jnp.repeat(jnp.exp(draws), shape[dim] // blocks).reshape((-1,) + (1,) * (len(shape) - dim - 1))

    factor_of = one(*pieces[0])
    for cut in pieces[1:]:
        factor_of = factor_of * one(*cut)
    return factor_of


def noise(stream_key, shape, deviation, limit, shards=(), kind=jnp.bfloat16):
    values = jax.random.normal(stream_key, shape, jnp.float32) * deviation
    if len(shards) > 0:
        values = block_levels(stream_key, shape, shards, -0.22, 0.18) * values
    return jnp.clip(values, min=-limit, max=limit).astype(kind)


def setup_inputs(seed: int = 0) -> dict:
    keys = jax.random.split(jax.random.key(seed), 7)
    return {
        "handed_on": noise(keys[0], (N_SECTION, N_DP, TOK, D), 1.0, 6.0, ((0, 8), (1, 4), (2, 8))),
        "handed_back": noise(keys[1], (N_SECTION, N_DP, TOK, D), 1.0, 6.0, ((0, 8), (1, 4), (2, 8))),
        "fresh": draw_fresh(jax.random.fold_in(keys[6], 71), 0),
        "evicted": draw_evicted(jax.random.fold_in(keys[6], 71), 0),
        "plan": set_ends(jax.random.randint(keys[4], (N_SECTION, N_DP), 0, SLOTS), jax.random.fold_in(keys[4], 1), 0, SLOTS - 1).astype(jnp.int32),
        "w_out": noise(keys[5], (N_SECTION, HEADS * HD, D), (HEADS * HD) ** -0.5, 0.078125, ((0, 8), (1, 8), (2, 4))),
    }


def attention_parts(packed):
    head_dim = packed.shape[-1] // 3
    length = packed.shape[0]
    scaling = 1.0 / math.sqrt(head_dim)
    queries = packed[..., :head_dim].astype(jnp.float32)
    key_rows = packed[..., head_dim:2 * head_dim].astype(jnp.float32)
    value_rows = packed[..., 2 * head_dim:].astype(jnp.float32)
    scores = jnp.einsum('qhd,khd->hqk', queries, key_rows) * scaling
    causal = jnp.arange(length)[:, None] >= jnp.arange(length)[None, :]
    scores = jnp.where(causal[None], scores, -1e+30)
    scores = scores - lax.optimization_barrier(jnp.max(scores, axis=-1, keepdims=True))
    weights = jnp.exp(scores)
    probs = weights / lax.optimization_barrier(jnp.sum(weights, axis=-1, keepdims=True))
    probs_low = probs.astype(jnp.bfloat16)
    attended = jnp.einsum('hqk,khd->qhd', probs_low.astype(jnp.float32), value_rows).astype(jnp.bfloat16)
    return (probs, probs_low, attended, queries, key_rows, value_rows, scaling)

def attention_backward(packed, d_attended):
    probs, probs_low, attended, queries, key_rows, value_rows, scaling = attention_parts(packed)
    d_high = d_attended.astype(jnp.float32)
    delta = jnp.einsum('qhd,qhd->hq', d_high, attended.astype(jnp.float32))
    d_values = jnp.einsum('hqk,qhd->khd', probs_low.astype(jnp.float32), d_high).astype(jnp.bfloat16)
    d_probs = jnp.einsum('qhd,khd->hqk', d_high, value_rows)
    d_scores = (probs * (d_probs - delta[:, :, None])).astype(jnp.bfloat16).astype(jnp.float32)
    d_queries = (jnp.einsum('hqk,khd->qhd', d_scores, key_rows) * scaling).astype(jnp.bfloat16)
    d_keys = (jnp.einsum('hqk,qhd->khd', d_scores, queries) * scaling).astype(jnp.bfloat16)
    return jnp.concatenate([d_queries, d_keys, d_values], axis=-1)

def reference(handed_on, handed_back, fresh, evicted, plan, w_out):
    sections = handed_on.shape[0]
    replicas = handed_on.shape[1]
    length = handed_on.shape[2]
    width = handed_on.shape[3]
    heads = fresh.shape[3]
    head_dim = fresh.shape[4] // 3
    group_width = heads // N_TENSOR * head_dim
    out_rows = []
    grad_rows = []
    for section in range(sections):
        weight = w_out[section]
        grouped = weight.reshape(N_TENSOR, group_width, width).astype(jnp.float32)
        outs_here = []
        grads_here = []
        for replica in range(replicas):
            incoming = handed_on[(section - 1) % sections, replica]
            upstream = handed_back[(section + 1) % sections, replica]
            attended = attention_parts(fresh[section, replica])[2].reshape(length, N_TENSOR, group_width)
            terms = jnp.einsum('tgk,gkd->gtd', attended.astype(jnp.float32), grouped).astype(jnp.bfloat16)
            terms = lax.optimization_barrier(terms)
            summed = lax.optimization_barrier(jnp.sum(terms.astype(jnp.float32), axis=0))
            outs_here.append((incoming.astype(jnp.float32) + summed).astype(jnp.bfloat16))
            d_attended = jnp.dot(upstream, weight.T, preferred_element_type=jnp.float32).astype(jnp.bfloat16)
            d_attended = d_attended.reshape(length, heads, head_dim)
            if section < sections // 2:
                slot = lax.dynamic_index_in_dim(evicted[sections - 1 - section], plan[section, replica].astype(jnp.int32), 0, keepdims=False)
                stored = slot[replica]
            else:
                stored = fresh[section, replica]
            grads_here.append(attention_backward(stored, d_attended))
        out_rows.append(jnp.stack(outs_here))
        grad_rows.append(jnp.stack(grads_here))
    return (jnp.stack(out_rows), jnp.stack(grad_rows))
```

```python
import math

import jax
import jax.numpy as jnp
from jax import lax
from jax.sharding import PartitionSpec as P

AXES = ("section", "tensor", "dp")
BF16 = jnp.bfloat16
F32 = jnp.float32


def attention_parts(packed):
    head_dim = packed.shape[-1] // 3
    length = packed.shape[0]
    scaling = 1.0 / math.sqrt(head_dim)
    queries = packed[..., :head_dim]
    key_rows = packed[..., head_dim : 2 * head_dim]
    value_rows = packed[..., 2 * head_dim :]
    scores = (
        jnp.einsum("qhd,khd->hqk", queries, key_rows, preferred_element_type=F32) * scaling
    )
    causal = jnp.arange(length)[:, None] >= jnp.arange(length)[None, :]
    scores = jnp.where(causal[None], scores, -1e30)
    scores = scores - jnp.max(scores, axis=-1, keepdims=True)
    weights = jnp.exp(scores)
    probs = weights / jnp.sum(weights, axis=-1, keepdims=True)
    probs_low = probs.astype(BF16)
    attended = jnp.einsum(
        "hqk,khd->qhd", probs_low, value_rows, preferred_element_type=F32
    ).astype(BF16)
    return (probs, probs_low, attended, queries, key_rows, value_rows, scaling)


def attention_backward(packed, d_attended):
    probs, probs_low, attended, queries, key_rows, value_rows, scaling = attention_parts(packed)
    delta = jnp.einsum("qhd,qhd->hq", d_attended, attended, preferred_element_type=F32)
    d_values = jnp.einsum(
        "hqk,qhd->khd", probs_low, d_attended, preferred_element_type=F32
    ).astype(BF16)
    d_probs = jnp.einsum("qhd,khd->hqk", d_attended, value_rows, preferred_element_type=F32)
    d_scores = (probs * (d_probs - delta[:, :, None])).astype(BF16)
    d_queries = (
        jnp.einsum("hqk,khd->qhd", d_scores, key_rows, preferred_element_type=F32) * scaling
    ).astype(BF16)
    d_keys = (
        jnp.einsum("hqk,qhd->khd", d_scores, queries, preferred_element_type=F32) * scaling
    ).astype(BF16)
    return jnp.concatenate([d_queries, d_keys, d_values], axis=-1)


def send(block, target):
    route = []
    for s in range(8):
        for zh in range(2):
            for y in range(4):
                for zl in range(4):
                    to = target(s, zh, y, zl)
                    if to is not None:
                        s2, zh2, y2, zl2 = to
                        there = (s2 % 8 * 8 + zh2 % 2 * 4 + y2 % 4) * 4 + zl2 % 4
                        route.append((((s * 2 + zh) * 4 + y) * 4 + zl, there))
    return lax.ppermute(block, AXES, route)


def rolled(array, amount, axis):
    array = jnp.where(amount % 2 == 1, jnp.roll(array, 1, axis), array)
    return jnp.where(amount // 2 == 1, jnp.roll(array, 2, axis), array)


def shards(handed_on, handed_back, fresh, evicted, plan, w_out):
    section = lax.axis_index("section")
    tensor = lax.axis_index("tensor")
    zl = lax.axis_index("dp")
    zh, y = tensor // 4, tensor % 4
    length, heads, width3 = fresh.shape[2:]
    rows, model = handed_on.shape[2:]
    weight = w_out[0]
    group_width, columns = weight.shape

    slot = send(plan, lambda s, zh, y, zl: (7 - s, zh, y, zl))[0, 0]
    picked = lax.dynamic_index_in_dim(evicted[0], slot, 0, keepdims=False)[0]
    fetched = send(picked, lambda s, zh, y, zl: (7 - s, zh, y, zl) if s >= 4 else None)
    stored = jnp.where(section < 4, fetched, fresh[0, 0])
    incoming = send(handed_on[0, 0], lambda s, zh, y, zl: (s + 1, zh, y, zl))

    gradient = handed_back[0, 0]
    lines = []
    for a in range(2):
        for j in range(4):
            block = lax.dynamic_slice_in_dim(gradient, (zl + j) % 4 * columns, columns, 1)
            lines.append(
                send(block, lambda s, zh, y, zl, a=a, j=j: (s - 1, zh ^ a, y, zl + j))
            )
    line = jnp.concatenate(lines, axis=0)

    def d_term(block):
        return lax.dot_general(
            block, weight, (((1,), (1,)), ((), ())), preferred_element_type=F32
        ).astype(BF16)

    d_rel = []
    for d in range(4):
        block = line if d == 0 else send(line, lambda s, zh, y, zl, d=d: (s, zh, y + d, zl))
        d_rel.append(d_term(block).reshape(2, 4, rows, group_width))
    d_rel = jnp.stack(d_rel)
    d_sum = d_rel[:, :, 0].astype(F32)
    for j in range(1, 4):
        d_sum += send(
            d_rel[:, :, j], lambda s, zh, y, zl, j=j: (s, zh, y, zl - j)
        ).astype(F32)
    d_sum = d_sum.astype(BF16)
    d_sum = rolled(d_sum[::-1], (y + 1) % 4, 0)
    d_sum = jnp.where(zh == 1, d_sum[:, ::-1], d_sum)
    d_attended = d_sum.transpose(1, 0, 2, 3).reshape(length, heads, width3 // 3)

    attended = attention_parts(fresh[0, 0])[2].reshape(2, 4, rows, group_width)
    attended = jnp.where(zh == 1, attended[::-1], attended)
    attended = rolled(attended, (4 - y) % 4, 1)
    replicas = [attended]
    for j in range(1, 4):
        replicas.append(send(attended, lambda s, zh, y, zl, j=j: (s, zh, y, zl + j)))
    together = jnp.stack(replicas, axis=2)
    total = None
    for d in (1, 3, 2, 0):
        term = jnp.dot(
            together[:, d].reshape(-1, group_width), weight, preferred_element_type=F32
        ).astype(BF16)
        if d:
            term = send(term, lambda s, zh, y, zl, d=d: (s, zh, y + d, zl))
        total = term.astype(F32) if total is None else total + term.astype(F32)
    total = total.astype(BF16).reshape(2, 4, rows, columns)
    outs = []
    for j in range(4):
        out = 0.0
        for a in range(2):
            term = total[a, j]
            if a or j:
                term = send(term, lambda s, zh, y, zl, a=a, j=j: (s, zh ^ a, y, zl - j))
            out = out + term.astype(F32)
        outs.append(out)
    out = rolled(jnp.stack(outs), zl, 0)
    out = out.transpose(1, 0, 2).reshape(rows, model)
    layer_out = (incoming.astype(F32) + out).astype(BF16)
    grads = attention_backward(stored, d_attended)
    return (layer_out[None, None], grads[None, None])


def solution(mesh):
    return jax.shard_map(
        shards,
        mesh=mesh,
        in_specs=(
            P("section", "dp", "tensor", None),
            P("section", "dp", "tensor", None),
            P("section", "dp", None, "tensor", None),
            P("section", None, "dp", None, "tensor", None),
            P("section", "dp"),
            P("section", "tensor", "dp"),
        ),
        out_specs=(P("section", "dp", "tensor", None), P("section", "dp", None, "tensor", None)),
        check_vma=False,
    )
```

```python
import functools
import math

import jax
import jax.numpy as jnp
from jax import lax
from jax.experimental import pallas as pl
from jax.experimental.pallas import tpu as pltpu
from jax.sharding import PartitionSpec as P

AXES = ("section", "tensor", "dp")
BF16 = jnp.bfloat16
F32 = jnp.float32
VMEM_LIMIT = 20 * 2**20
AHEAD = 40 * 10**6


def send(block, target):
    route = []
    for s in range(8):
        for zh in range(2):
            for y in range(4):
                for zl in range(4):
                    to = target(s, zh, y, zl)
                    if to is not None:
                        s2, zh2, y2, zl2 = to
                        there = (s2 % 8 * 8 + zh2 % 2 * 4 + y2 % 4) * 4 + zl2 % 4
                        route.append((((s * 2 + zh) * 4 + y) * 4 + zl, there))
    return lax.ppermute(block, AXES, route)


def call(kernel, out_shapes, place, *arrays, scratch=(), weighed=0):
    return pl.pallas_call(
        kernel,
        out_shape=[
            shape if isinstance(shape, jax.ShapeDtypeStruct) else jax.ShapeDtypeStruct(shape, BF16)
            for shape in out_shapes
        ],
        in_specs=[pl.BlockSpec(memory_space=pltpu.SMEM)]
        + [pl.BlockSpec(memory_space=pltpu.VMEM)] * len(arrays),
        out_specs=[pl.BlockSpec(memory_space=pltpu.VMEM)] * len(out_shapes),
        scratch_shapes=[pltpu.VMEM(shape, BF16) for shape in scratch],
        compiler_params=pltpu.CompilerParams(vmem_limit_bytes=VMEM_LIMIT),
        cost_estimate=pl.CostEstimate(flops=0, bytes_accessed=weighed, transcendentals=0),
    )(place, *arrays)


def dot(a, b, contract):
    return lax.dot_general(a, b, (contract, ((), ())), preferred_element_type=F32)


NN = ((1,), (0,))
NT = ((1,), (1,))
TN = ((0,), (0,))


def probabilities(queries, key_rows):
    length, head_dim = queries.shape
    scores = dot(queries, key_rows, NT) * (1.0 / math.sqrt(head_dim))
    causal = lax.broadcasted_iota(jnp.int32, (length, length), 0) >= lax.broadcasted_iota(
        jnp.int32, (length, length), 1
    )
    scores = jnp.where(causal, scores, -1e30)
    weights = jnp.exp(scores - jnp.max(scores, axis=-1, keepdims=True))
    return weights * (1.0 / jnp.sum(weights, axis=-1, keepdims=True))


def forward_kernel(place, packed, out):
    zh, y = place[1], place[2]
    heads, length, width = packed.shape
    hd = width // 3
    rows = length // 8
    for h in range(heads):
        probs = probabilities(packed[h, :, :hd], packed[h, :, hd : 2 * hd])
        attended = dot(probs.astype(BF16), packed[h, :, 2 * hd :], NN).astype(BF16)
        for b in range(2):
            for c in range(4):
                at = (b * 4 + c) * rows
                out[(c - y) & 3, b ^ zh, :, h * hd : (h + 1) * hd] = attended[at : at + rows]


def stored_kernel(place, fetched, fresh, stored, probs, attended):
    section = place[0]
    heads, length, width = fetched.shape
    hd = width // 3
    for h in range(heads):
        packed = jnp.where(section < 4, fetched[h], fresh[h])
        stored[h] = packed
        probs[h] = probabilities(packed[:, :hd], packed[:, hd : 2 * hd])
        attended[h] = dot(probs[h].astype(BF16), packed[:, 2 * hd :], NN).astype(BF16)


def backward_kernel(place, stored, probs, attended, *refs):
    zh, y = place[1], place[2]
    terms, out, scratch = refs[:4], refs[4], refs[5]
    heads, length, width = stored.shape
    hd = width // 3
    scaling = 1.0 / math.sqrt(hd)
    scratch[...] = sum(ref[...].astype(F32) for ref in terms).astype(BF16)
    for h in range(heads):
        queries = stored[h, :, :hd]
        key_rows = stored[h, :, hd : 2 * hd]
        value_rows = stored[h, :, 2 * hd :]
        d_attended = jnp.concatenate(
            [
                scratch[(y - c) & 3, b ^ zh, :, h * hd : (h + 1) * hd]
                for b in range(2)
                for c in range(4)
            ],
            axis=0,
        )
        probs_low = probs[h].astype(BF16)
        delta = jnp.sum(
            d_attended.astype(F32) * attended[h].astype(F32), axis=-1, keepdims=True
        )
        d_values = dot(probs_low, d_attended, TN).astype(BF16)
        d_probs = dot(d_attended, value_rows, NT)
        d_scores = (probs[h] * (d_probs - delta)).astype(BF16)
        out[h, :, :hd] = (dot(d_scores, key_rows, NN) * scaling).astype(BF16)
        out[h, :, hd : 2 * hd] = (dot(d_scores, queries, TN) * scaling).astype(BF16)
        out[h, :, 2 * hd :] = d_values


def term_kernel(place, *refs, d, cuts):
    pieces, weight, outs = refs[:4], refs[4], refs[5:]
    left = jnp.concatenate([piece[d, a] for a in range(2) for piece in pieces])
    width = 512
    rows = left.shape[0] // cuts
    for at in range(0, weight.shape[1], width):
        product = dot(left, weight[:, at : at + width], NN).astype(BF16)
        for i, out in enumerate(outs):
            out[:, at : at + width] = product[i * rows : (i + 1) * rows]


def gradient_kernel(place, *refs):
    pieces, weight, out = refs[:-2], refs[-2], refs[-1]
    width = 256
    for at in range(0, out.shape[1], width):
        row = 0
        for piece in pieces:
            rows = piece.shape[0]
            out[row : row + rows, at : at + width] = dot(
                piece[...], weight[at : at + width], NT
            ).astype(BF16)
            row += rows


def columns_kernel(place, gradient, weight, *outs):
    zl = place[3]
    width = outs[0].shape[1]
    for j, out in enumerate(outs):
        out[...] = gradient[:, pl.ds(pl.multiple_of(((zl + j) & 3) * width, width), width)]


def second_kernel(place, above, below, from_below, from_above, *refs):
    lines, (out_above, out_below, line) = refs[:4], refs[4:]
    half = from_below.shape[0]
    top, bottom = slice(0, half), slice(half, 2 * half)
    out_above[top] = (above[top].astype(F32) + from_below[...].astype(F32)).astype(BF16)
    out_above[bottom] = above[bottom]
    out_below[top] = below[top]
    out_below[bottom] = (below[bottom].astype(F32) + from_above[...].astype(F32)).astype(BF16)
    rows = lines[0].shape[0]
    for i, ref in enumerate(lines):
        line[i * rows : (i + 1) * rows] = ref[...]


def stack_kernel(place, *refs):
    out = refs[-1]
    rows = refs[0].shape[0]
    for i, ref in enumerate(refs[:-1]):
        out[i * rows : (i + 1) * rows] = ref[...]


def third_kernel(place, own, left, right, kept, given):
    half = kept.shape[0]
    for at, out in ((slice(0, half), kept), (slice(half, 2 * half), given)):
        out[...] = (
            own[at].astype(F32) + left[at].astype(F32) + right[at].astype(F32)
        ).astype(BF16)


def pair_kernel(place, one, other, *outs):
    rows = outs[0].shape[0]
    for i, out in enumerate(outs):
        at = slice(i * rows, (i + 1) * rows)
        out[...] = (one[at].astype(F32) + other[at].astype(F32)).astype(BF16)


def halves_kernel(place, left, right, top, bottom):
    half = top.shape[0]
    top[...] = left[:half]
    bottom[...] = right[half:]


def output_kernel(place, incoming, *refs):
    zl = place[3]
    terms, out = refs[:4], refs[4]
    width = terms[0].shape[1]
    for j, term in enumerate(terms):
        at = pl.ds(pl.multiple_of(((zl + j) & 3) * width, width), width)
        out[:, at] = (incoming[:, at].astype(F32) + term[...].astype(F32)).astype(BF16)


def after(values, *others):
    flat = [leaf for other in others for leaf in other]
    return lax.optimization_barrier((*values, *flat))[: len(values)]


def shards(handed_on, handed_back, fresh, evicted, plan, w_out):
    section = lax.axis_index("section")
    tensor = lax.axis_index("tensor")
    zl = lax.axis_index("dp")
    zh, y = tensor >> 2, tensor & 3
    place = jnp.stack([section, zh, y, zl]).astype(jnp.int32)
    length, heads, width3 = fresh.shape[2:]
    rows, model = handed_on.shape[2:]
    weight = w_out[0]
    group_width, columns = weight.shape
    fresh_heads = fresh[0, 0].transpose(1, 0, 2)
    wide = (rows, columns)
    block = (2, rows, group_width)
    half = 4 * rows
    up = lambda s, zh, y, zl: (s, zh, y + 1, zl)
    down = lambda s, zh, y, zl: (s, zh, y - 1, zl)

    swap = lambda s, zh, y, zl: (s, zh ^ 1, y, zl)

    slot = send(plan, lambda s, zh, y, zl: (7 - s, zh, y, zl))
    attended = call(forward_kernel, [(4, *block)], place, fresh_heads)[0]
    attended, slot = after([attended, slot])
    replicas = [attended] + [
        send(attended, lambda s, zh, y, zl, j=j: (s, zh, y, zl + j)) for j in range(1, 4)
    ]
    upstream = send(handed_back[0, 0], lambda s, zh, y, zl: (s - 1, zh, y, zl))
    incoming = send(handed_on[0, 0], lambda s, zh, y, zl: (s + 1, zh, y, zl))
    picked = lax.dynamic_index_in_dim(evicted[0], slot[0, 0], 0, keepdims=False)[0]
    blocks = call(columns_kernel, [wide] * 4, place, upstream, weight)
    picked, incoming, *rest = after([picked.transpose(1, 0, 2), incoming, *replicas, *blocks])
    replicas, blocks = rest[:4], rest[4:]

    def term(d, cuts=1):
        kernel = functools.partial(term_kernel, d=d, cuts=cuts)
        return call(kernel, [(8 * rows // cuts, columns)] * cuts, place, *replicas, weight)

    top, bottom, *blocks = after([*term(2, 2), *blocks])
    from_below, from_above = send(top, up), send(bottom, down)
    lines = [blocks[0]] + [
        send(blocks[j], lambda s, zh, y, zl, j=j: (s, zh, y, zl + j)) for j in range(1, 4)
    ]
    above, below = term(1)[0], term(3)[0]
    above, below, from_below, from_above, *lines = after(
        [above, below, from_below, from_above, *lines]
    )

    tall = (2 * half, columns)
    above, below, line0 = call(
        second_kernel,
        [tall, tall, (half, columns)],
        place,
        above,
        below,
        from_below,
        from_above,
        *lines,
    )
    above, below, line0 = after([above, below, line0])
    from_below, from_above = send(above, up), send(below, down)
    line1 = send(line0, swap)
    fetched = send(picked, lambda s, zh, y, zl: (7 - s, zh, y, zl) if s >= 4 else None)
    own = term(0)[0]
    line = call(stack_kernel, [tall], place, line0, line1, weighed=AHEAD)[0]
    own, from_below, from_above, line, fetched = after(
        [own, from_below, from_above, line, fetched]
    )

    kept, given = call(third_kernel, [(half, columns)] * 2, place, own, from_below, from_above)
    line, kept, given = after([line, kept, given])
    left, right = send(line, up), send(line, down)
    given = send(given, swap)

    def d_term(*pieces):
        return call(gradient_kernel, [(8 * rows, group_width)], place, *pieces, weight)[0]

    stored = call(
        stored_kernel,
        [
            (heads, length, width3),
            jax.ShapeDtypeStruct((heads, length, length), F32),
            (heads, length, group_width // heads),
        ],
        place,
        fetched,
        fresh_heads,
    )
    near0 = d_term(line)
    terms = call(pair_kernel, [wide] * 4, place, kept, given, weighed=AHEAD)
    left, right, near0, *rest = after([left, right, near0, *terms, *stored])
    terms, stored = rest[:4], rest[4:]

    top, bottom = call(halves_kernel, [(half, columns)] * 2, place, left, right)
    top, bottom, *terms = after([top, bottom, *terms])
    across = [send(top, up), send(bottom, down)]
    terms = [terms[0]] + [
        send(terms[j], lambda s, zh, y, zl, j=j: (s, zh, y, zl - j)) for j in range(1, 4)
    ]
    near1, near3 = d_term(left), d_term(right)
    near1, near3, *rest = after([near1, near3, *across, *terms])
    across, terms = rest[:2], rest[2:]

    near2 = dot(jnp.concatenate(across), weight, NT).astype(BF16)
    d_rel = jnp.stack([near0, near1, near2, near3]).reshape(4, 2, 4, rows, group_width)
    d_terms = [d_rel[:, :, 0]] + [
        send(d_rel[:, :, j], lambda s, zh, y, zl, j=j: (s, zh, y, zl - j)) for j in range(1, 4)
    ]
    layer_out = call(output_kernel, [(rows, model)], place, incoming, *terms)[0]
    grads = call(
        backward_kernel,
        [(heads, length, width3)],
        place,
        *stored,
        *d_terms,
        scratch=[(4, *block)],
    )[0]
    return (layer_out[None, None], grads.transpose(1, 0, 2)[None, None])


def solution(mesh):
    return jax.shard_map(
        shards,
        mesh=mesh,
        in_specs=(
            P("section", "dp", "tensor", None),
            P("section", "dp", "tensor", None),
            P("section", "dp", None, "tensor", None),
            P("section", None, "dp", None, "tensor", None),
            P("section", "dp"),
            P("section", "tensor", "dp"),
        ),
        out_specs=(P("section", "dp", "tensor", None), P("section", "dp", None, "tensor", None)),
        check_vma=False,
    )
```

```python
import functools
import math

import jax
import jax.numpy as jnp
from jax import lax
from jax.experimental import pallas as pl
from jax.experimental.pallas import tpu as pltpu
from jax.sharding import PartitionSpec as P

AXES = ("section", "tensor", "dp")
BF16 = jnp.bfloat16
F32 = jnp.float32
VMEM_LIMIT = 20 * 2**20


def send(block, target):
    route = []
    for s in range(8):
        for zh in range(2):
            for y in range(4):
                for zl in range(4):
                    to = target(s, zh, y, zl)
                    if to is not None:
                        s2, zh2, y2, zl2 = to
                        there = (s2 % 8 * 8 + zh2 % 2 * 4 + y2 % 4) * 4 + zl2 % 4
                        route.append((((s * 2 + zh) * 4 + y) * 4 + zl, there))
    return lax.ppermute(block, AXES, route)


def call(kernel, out_shapes, place, *arrays, scratch=()):
    return pl.pallas_call(
        kernel,
        out_shape=[
            shape if isinstance(shape, jax.ShapeDtypeStruct) else jax.ShapeDtypeStruct(shape, BF16)
            for shape in out_shapes
        ],
        in_specs=[pl.BlockSpec(memory_space=pltpu.SMEM)]
        + [pl.BlockSpec(memory_space=pltpu.VMEM)] * len(arrays),
        out_specs=[pl.BlockSpec(memory_space=pltpu.VMEM)] * len(out_shapes),
        scratch_shapes=[pltpu.VMEM(shape, BF16) for shape in scratch],
        compiler_params=pltpu.CompilerParams(vmem_limit_bytes=VMEM_LIMIT),
        cost_estimate=pl.CostEstimate(flops=0, bytes_accessed=0, transcendentals=0),
    )(place, *arrays)


def dot(a, b, contract):
    return lax.dot_general(a, b, (contract, ((), ())), preferred_element_type=F32)


NN = ((1,), (0,))
NT = ((1,), (1,))
TN = ((0,), (0,))


def probabilities(queries, key_rows):
    length, head_dim = queries.shape
    scores = dot(queries, key_rows, NT) * (1.0 / math.sqrt(head_dim))
    causal = lax.broadcasted_iota(jnp.int32, (length, length), 0) >= lax.broadcasted_iota(
        jnp.int32, (length, length), 1
    )
    scores = jnp.where(causal, scores, -1e30)
    weights = jnp.exp(scores - jnp.max(scores, axis=-1, keepdims=True))
    return weights * (1.0 / jnp.sum(weights, axis=-1, keepdims=True))


def forward_kernel(place, packed, out):
    zh, y = place[1], place[2]
    heads, length, width = packed.shape
    hd = width // 3
    rows = length // 8
    for h in range(heads):
        probs = probabilities(packed[h, :, :hd], packed[h, :, hd : 2 * hd])
        attended = dot(probs.astype(BF16), packed[h, :, 2 * hd :], NN).astype(BF16)
        for b in range(2):
            for c in range(4):
                at = (b * 4 + c) * rows
                out[(c - y) & 3, b ^ zh, :, h * hd : (h + 1) * hd] = attended[at : at + rows]


def stored_kernel(place, fetched, fresh, stored, probs, attended):
    section = place[0]
    heads, length, width = fetched.shape
    hd = width // 3
    for h in range(heads):
        packed = jnp.where(section < 4, fetched[h], fresh[h])
        stored[h] = packed
        probs[h] = probabilities(packed[:, :hd], packed[:, hd : 2 * hd])
        attended[h] = dot(probs[h].astype(BF16), packed[:, 2 * hd :], NN).astype(BF16)


def backward_kernel(place, stored, probs, attended, *refs):
    zh, y = place[1], place[2]
    terms, out, scratch = refs[:4], refs[4], refs[5]
    heads, length, width = stored.shape
    hd = width // 3
    scaling = 1.0 / math.sqrt(hd)
    scratch[...] = sum(ref[...].astype(F32) for ref in terms).astype(BF16)
    for h in range(heads):
        queries = stored[h, :, :hd]
        key_rows = stored[h, :, hd : 2 * hd]
        value_rows = stored[h, :, 2 * hd :]
        d_attended = jnp.concatenate(
            [
                scratch[(y - c) & 3, b ^ zh, :, h * hd : (h + 1) * hd]
                for b in range(2)
                for c in range(4)
            ],
            axis=0,
        )
        probs_low = probs[h].astype(BF16)
        delta = jnp.sum(
            d_attended.astype(F32) * attended[h].astype(F32), axis=-1, keepdims=True
        )
        d_values = dot(probs_low, d_attended, TN).astype(BF16)
        d_probs = dot(d_attended, value_rows, NT)
        d_scores = (probs[h] * (d_probs - delta)).astype(BF16)
        out[h, :, :hd] = (dot(d_scores, key_rows, NN) * scaling).astype(BF16)
        out[h, :, hd : 2 * hd] = (dot(d_scores, queries, TN) * scaling).astype(BF16)
        out[h, :, 2 * hd :] = d_values


def term_kernel(place, *refs, d, cuts):
    pieces, weight, outs = refs[:4], refs[4], refs[5:]
    left = jnp.concatenate([piece[d, a] for a in range(2) for piece in pieces])
    width = 512
    rows = left.shape[0] // cuts
    for at in range(0, weight.shape[1], width):
        product = dot(left, weight[:, at : at + width], NN).astype(BF16)
        for i, out in enumerate(outs):
            out[:, at : at + width] = product[i * rows : (i + 1) * rows]


def gradient_kernel(place, *refs):
    pieces, weight, out = refs[:-2], refs[-2], refs[-1]
    width = 256
    for at in range(0, out.shape[1], width):
        row = 0
        for piece in pieces:
            rows = piece.shape[0]
            out[row : row + rows, at : at + width] = dot(
                piece[...], weight[at : at + width], NT
            ).astype(BF16)
            row += rows


def columns_kernel(place, gradient, weight, *outs):
    zl = place[3]
    width = outs[0].shape[1]
    for j, out in enumerate(outs):
        out[...] = gradient[:, pl.ds(pl.multiple_of(((zl + j) & 3) * width, width), width)]


def second_kernel(place, above, below, from_below, from_above, *refs):
    lines, (out_above, out_below, line) = refs[:4], refs[4:]
    half = from_below.shape[0]
    top, bottom = slice(0, half), slice(half, 2 * half)
    out_above[top] = (above[top].astype(F32) + from_below[...].astype(F32)).astype(BF16)
    out_above[bottom] = above[bottom]
    out_below[top] = below[top]
    out_below[bottom] = (below[bottom].astype(F32) + from_above[...].astype(F32)).astype(BF16)
    rows = lines[0].shape[0]
    for i, ref in enumerate(lines):
        line[i * rows : (i + 1) * rows] = ref[...]


def stack_kernel(place, *refs):
    out = refs[-1]
    at = 0
    for ref in refs[:-1]:
        rows = ref.shape[0]
        out[at : at + rows] = ref[...]
        at += rows


def third_kernel(place, own, left, right, *outs):
    rows = outs[0].shape[0]
    for i, out in enumerate(outs):
        at = slice(i * rows, (i + 1) * rows)
        out[...] = (
            own[at].astype(F32) + left[at].astype(F32) + right[at].astype(F32)
        ).astype(BF16)


def pair_kernel(place, one, other, *outs):
    rows = outs[0].shape[0]
    for i, out in enumerate(outs):
        at = slice(i * rows, (i + 1) * rows)
        out[...] = (one[at].astype(F32) + other[at].astype(F32)).astype(BF16)


def halves_kernel(place, left, right, top, bottom):
    half = top.shape[0]
    top[...] = left[:half]
    bottom[...] = right[half:]


def output_kernel(place, incoming, *refs):
    zl = place[3]
    terms, out = refs[:4], refs[4]
    width = terms[0].shape[1]
    for j, term in enumerate(terms):
        at = pl.ds(pl.multiple_of(((zl + j) & 3) * width, width), width)
        out[:, at] = (incoming[:, at].astype(F32) + term[...].astype(F32)).astype(BF16)


def after(values, *others):
    flat = [leaf for other in others for leaf in other]
    return lax.optimization_barrier((*values, *flat))[: len(values)]


def shards(handed_on, handed_back, fresh, evicted, plan, w_out):
    section = lax.axis_index("section")
    tensor = lax.axis_index("tensor")
    zl = lax.axis_index("dp")
    zh, y = tensor >> 2, tensor & 3
    place = jnp.stack([section, zh, y, zl]).astype(jnp.int32)
    length, heads, width3 = fresh.shape[2:]
    rows, model = handed_on.shape[2:]
    weight = w_out[0]
    group_width, columns = weight.shape
    fresh_heads = fresh[0, 0].transpose(1, 0, 2)
    wide = (rows, columns)
    block = (2, rows, group_width)
    half = 4 * rows
    up = lambda s, zh, y, zl: (s, zh, y + 1, zl)
    down = lambda s, zh, y, zl: (s, zh, y - 1, zl)

    slot = send(plan, lambda s, zh, y, zl: (7 - s, zh, y, zl))
    attended = call(forward_kernel, [(4, *block)], place, fresh_heads)[0]
    replicas = [attended] + [
        send(attended, lambda s, zh, y, zl, j=j: (s, zh, y, zl + j)) for j in range(1, 4)
    ]
    upstream = send(handed_back[0, 0], lambda s, zh, y, zl: (s - 1, zh, y, zl))
    incoming = send(handed_on[0, 0], lambda s, zh, y, zl: (s + 1, zh, y, zl))
    upstream, slot = after([upstream, slot], [attended])
    picked = lax.dynamic_index_in_dim(evicted[0], slot[0, 0], 0, keepdims=False)[0]
    blocks = call(columns_kernel, [wide] * 4, place, upstream, weight)
    picked, incoming, *rest = after([picked.transpose(1, 0, 2), incoming, *replicas, *blocks])
    replicas, blocks = rest[:4], rest[4:]

    def term(d, cuts=1):
        kernel = functools.partial(term_kernel, d=d, cuts=cuts)
        return call(kernel, [(8 * rows // cuts, columns)] * cuts, place, *replicas, weight)

    top, bottom, *blocks = after([*term(2, 2), *blocks])
    from_below, from_above = send(top, up), send(bottom, down)
    lines = [blocks[0]] + [
        send(blocks[j], lambda s, zh, y, zl, j=j: (s, zh, y, zl + j)) for j in range(1, 4)
    ]
    above, below = term(1)[0], term(3)[0]
    above, below, from_below, from_above, *lines = after(
        [above, below, from_below, from_above, *lines]
    )

    tall = (2 * half, columns)
    above, below, line0 = call(
        second_kernel,
        [tall, tall, (half, columns)],
        place,
        above,
        below,
        from_below,
        from_above,
        *lines,
    )
    above, below, line0, *blocks = after([above, below, line0, *blocks])
    from_below, from_above = send(above, up), send(below, down)
    lines = [
        send(blocks[j], lambda s, zh, y, zl, j=j: (s, zh ^ 1, y, zl + j)) for j in range(4)
    ]
    own = term(0)[0]
    line = call(stack_kernel, [tall], place, line0, *lines)[0]
    own, from_below, from_above, line = after([own, from_below, from_above, line])

    kept, given = call(third_kernel, [(half, columns)] * 2, place, own, from_below, from_above)
    line, kept, given = after([line, kept, given])
    left, right = send(line, up), send(line, down)
    given = send(given, lambda s, zh, y, zl: (s, zh ^ 1, y, zl))

    def d_term(*pieces):
        return call(gradient_kernel, [(8 * rows, group_width)], place, *pieces, weight)[0]

    fetched = send(picked, lambda s, zh, y, zl: (7 - s, zh, y, zl) if s >= 4 else None)
    near0 = d_term(line)
    terms = call(pair_kernel, [wide] * 4, place, kept, given)
    left, right, near0, fetched, *terms = after([left, right, near0, fetched, *terms])

    top, bottom = call(halves_kernel, [(half, columns)] * 2, place, left, right)
    top, bottom, *terms = after([top, bottom, *terms])
    across = [send(top, up), send(bottom, down)]
    stored = call(
        stored_kernel,
        [
            (heads, length, width3),
            jax.ShapeDtypeStruct((heads, length, length), F32),
            (heads, length, group_width // heads),
        ],
        place,
        fetched,
        fresh_heads,
    )
    terms = [terms[0]] + [
        send(terms[j], lambda s, zh, y, zl, j=j: (s, zh, y, zl - j)) for j in range(1, 4)
    ]
    near1, near3 = d_term(left), d_term(right)
    near1, near3, *rest = after([near1, near3, *across, *terms], stored)
    across, terms = rest[:2], rest[2:]

    near2 = dot(jnp.concatenate(across), weight, NT).astype(BF16)
    d_rel = jnp.stack([near0, near1, near2, near3]).reshape(4, 2, 4, rows, group_width)
    d_terms = [d_rel[:, :, 0]] + [
        send(d_rel[:, :, j], lambda s, zh, y, zl, j=j: (s, zh, y, zl - j)) for j in range(1, 4)
    ]
    layer_out = call(output_kernel, [(rows, model)], place, incoming, *terms)[0]
    grads = call(
        backward_kernel,
        [(heads, length, width3)],
        place,
        *stored,
        *d_terms,
        scratch=[(4, *block)],
    )[0]
    return (layer_out[None, None], grads.transpose(1, 0, 2)[None, None])


def solution(mesh):
    return jax.shard_map(
        shards,
        mesh=mesh,
        in_specs=(
            P("section", "dp", "tensor", None),
            P("section", "dp", "tensor", None),
            P("section", "dp", None, "tensor", None),
            P("section", None, "dp", None, "tensor", None),
            P("section", "dp"),
            P("section", "tensor", "dp"),
        ),
        out_specs=(P("section", "dp", "tensor", None), P("section", "dp", None, "tensor", None)),
        check_vma=False,
    )
```

```python
import functools
import math

import jax
import jax.numpy as jnp
from jax import lax
from jax.experimental import pallas as pl
from jax.experimental.pallas import tpu as pltpu
from jax.sharding import PartitionSpec as P

AXES = ("section", "tensor", "dp")
BF16 = jnp.bfloat16
F32 = jnp.float32
VMEM_LIMIT = 20 * 2**20


def send(block, target):
    route = []
    for s in range(8):
        for zh in range(2):
            for y in range(4):
                for zl in range(4):
                    to = target(s, zh, y, zl)
                    if to is not None:
                        s2, zh2, y2, zl2 = to
                        there = (s2 % 8 * 8 + zh2 % 2 * 4 + y2 % 4) * 4 + zl2 % 4
                        route.append((((s * 2 + zh) * 4 + y) * 4 + zl, there))
    return lax.ppermute(block, AXES, route)


def call(kernel, out_shapes, place, *arrays, scratch=()):
    return pl.pallas_call(
        kernel,
        out_shape=[
            shape if isinstance(shape, jax.ShapeDtypeStruct) else jax.ShapeDtypeStruct(shape, BF16)
            for shape in out_shapes
        ],
        in_specs=[pl.BlockSpec(memory_space=pltpu.SMEM)]
        + [pl.BlockSpec(memory_space=pltpu.VMEM)] * len(arrays),
        out_specs=[pl.BlockSpec(memory_space=pltpu.VMEM)] * len(out_shapes),
        scratch_shapes=[pltpu.VMEM(shape, BF16) for shape in scratch],
        compiler_params=pltpu.CompilerParams(vmem_limit_bytes=VMEM_LIMIT),
        cost_estimate=pl.CostEstimate(flops=0, bytes_accessed=0, transcendentals=0),
    )(place, *arrays)


def dot(a, b, contract):
    return lax.dot_general(a, b, (contract, ((), ())), preferred_element_type=F32)


NN = ((1,), (0,))
NT = ((1,), (1,))
TN = ((0,), (0,))


def probabilities(queries, key_rows):
    length, head_dim = queries.shape
    scores = dot(queries, key_rows, NT) * (1.0 / math.sqrt(head_dim))
    causal = lax.broadcasted_iota(jnp.int32, (length, length), 0) >= lax.broadcasted_iota(
        jnp.int32, (length, length), 1
    )
    scores = jnp.where(causal, scores, -1e30)
    weights = jnp.exp(scores - jnp.max(scores, axis=-1, keepdims=True))
    return weights * (1.0 / jnp.sum(weights, axis=-1, keepdims=True))


def forward_kernel(place, packed, out):
    zh, y = place[1], place[2]
    heads, length, width = packed.shape
    hd = width // 3
    rows = length // 8
    for h in range(heads):
        probs = probabilities(packed[h, :, :hd], packed[h, :, hd : 2 * hd])
        attended = dot(probs.astype(BF16), packed[h, :, 2 * hd :], NN).astype(BF16)
        for b in range(2):
            for c in range(4):
                at = (b * 4 + c) * rows
                out[(c - y) & 3, b ^ zh, :, h * hd : (h + 1) * hd] = attended[at : at + rows]


def stored_kernel(place, fetched, fresh, stored, probs, attended):
    section = place[0]
    heads, length, width = fetched.shape
    hd = width // 3
    for h in range(heads):
        packed = jnp.where(section < 4, fetched[h], fresh[h])
        stored[h] = packed
        probs[h] = probabilities(packed[:, :hd], packed[:, hd : 2 * hd])
        attended[h] = dot(probs[h].astype(BF16), packed[:, 2 * hd :], NN).astype(BF16)


def backward_kernel(place, stored, probs, attended, *refs):
    zh, y = place[1], place[2]
    terms, out, scratch = refs[:4], refs[4], refs[5]
    heads, length, width = stored.shape
    hd = width // 3
    scaling = 1.0 / math.sqrt(hd)
    scratch[...] = sum(ref[...].astype(F32) for ref in terms).astype(BF16)
    for h in range(heads):
        queries = stored[h, :, :hd]
        key_rows = stored[h, :, hd : 2 * hd]
        value_rows = stored[h, :, 2 * hd :]
        d_attended = jnp.concatenate(
            [
                scratch[(y - c) & 3, b ^ zh, :, h * hd : (h + 1) * hd]
                for b in range(2)
                for c in range(4)
            ],
            axis=0,
        )
        probs_low = probs[h].astype(BF16)
        delta = jnp.sum(
            d_attended.astype(F32) * attended[h].astype(F32), axis=-1, keepdims=True
        )
        d_values = dot(probs_low, d_attended, TN).astype(BF16)
        d_probs = dot(d_attended, value_rows, NT)
        d_scores = (probs[h] * (d_probs - delta)).astype(BF16)
        out[h, :, :hd] = (dot(d_scores, key_rows, NN) * scaling).astype(BF16)
        out[h, :, hd : 2 * hd] = (dot(d_scores, queries, TN) * scaling).astype(BF16)
        out[h, :, 2 * hd :] = d_values


def term_kernel(place, *refs, d, cuts):
    pieces, weight, outs = refs[:4], refs[4], refs[5:]
    left = jnp.concatenate([piece[d, a] for a in range(2) for piece in pieces])
    width = 512
    rows = left.shape[0] // cuts
    for at in range(0, weight.shape[1], width):
        product = dot(left, weight[:, at : at + width], NN).astype(BF16)
        for i, out in enumerate(outs):
            out[:, at : at + width] = product[i * rows : (i + 1) * rows]


def gradient_kernel(place, *refs):
    pieces, weight, out = refs[:-2], refs[-2], refs[-1]
    width = 256
    for at in range(0, out.shape[1], width):
        row = 0
        for piece in pieces:
            rows = piece.shape[0]
            out[row : row + rows, at : at + width] = dot(
                piece[...], weight[at : at + width], NT
            ).astype(BF16)
            row += rows


def columns_kernel(place, gradient, weight, *outs):
    zl = place[3]
    width = outs[0].shape[1]
    for j, out in enumerate(outs):
        out[...] = gradient[:, pl.ds(pl.multiple_of(((zl + j) & 3) * width, width), width)]


def second_kernel(place, above, below, from_below, from_above, *refs):
    lines, (out_above, out_below, line) = refs[:4], refs[4:]
    half = from_below.shape[0]
    top, bottom = slice(0, half), slice(half, 2 * half)
    out_above[top] = (above[top].astype(F32) + from_below[...].astype(F32)).astype(BF16)
    out_above[bottom] = above[bottom]
    out_below[top] = below[top]
    out_below[bottom] = (below[bottom].astype(F32) + from_above[...].astype(F32)).astype(BF16)
    rows = lines[0].shape[0]
    for i, ref in enumerate(lines):
        line[i * rows : (i + 1) * rows] = ref[...]


def stack_kernel(place, *refs):
    out = refs[-1]
    at = 0
    for ref in refs[:-1]:
        rows = ref.shape[0]
        out[at : at + rows] = ref[...]
        at += rows


def third_kernel(place, own, left, right, *outs):
    rows = outs[0].shape[0]
    for i, out in enumerate(outs):
        at = slice(i * rows, (i + 1) * rows)
        out[...] = (
            own[at].astype(F32) + left[at].astype(F32) + right[at].astype(F32)
        ).astype(BF16)


def pair_kernel(place, one, other, *outs):
    rows = outs[0].shape[0]
    for i, out in enumerate(outs):
        at = slice(i * rows, (i + 1) * rows)
        out[...] = (one[at].astype(F32) + other[at].astype(F32)).astype(BF16)


def halves_kernel(place, left, right, top, bottom):
    half = top.shape[0]
    top[...] = left[:half]
    bottom[...] = right[half:]


def output_kernel(place, incoming, *refs):
    zl = place[3]
    terms, out = refs[:4], refs[4]
    width = terms[0].shape[1]
    for j, term in enumerate(terms):
        at = pl.ds(pl.multiple_of(((zl + j) & 3) * width, width), width)
        out[:, at] = (incoming[:, at].astype(F32) + term[...].astype(F32)).astype(BF16)


def after(values, *others):
    flat = [leaf for other in others for leaf in other]
    return lax.optimization_barrier((*values, *flat))[: len(values)]


def shards(handed_on, handed_back, fresh, evicted, plan, w_out):
    section = lax.axis_index("section")
    tensor = lax.axis_index("tensor")
    zl = lax.axis_index("dp")
    zh, y = tensor >> 2, tensor & 3
    place = jnp.stack([section, zh, y, zl]).astype(jnp.int32)
    length, heads, width3 = fresh.shape[2:]
    rows, model = handed_on.shape[2:]
    weight = w_out[0]
    group_width, columns = weight.shape
    fresh_heads = fresh[0, 0].transpose(1, 0, 2)
    wide = (rows, columns)
    block = (2, rows, group_width)
    half = 4 * rows
    up = lambda s, zh, y, zl: (s, zh, y + 1, zl)
    down = lambda s, zh, y, zl: (s, zh, y - 1, zl)

    slot = send(plan, lambda s, zh, y, zl: (7 - s, zh, y, zl))
    attended = call(forward_kernel, [(4, *block)], place, fresh_heads)[0]
    replicas = [attended] + [
        send(attended, lambda s, zh, y, zl, j=j: (s, zh, y, zl + j)) for j in range(1, 4)
    ]
    upstream = send(handed_back[0, 0], lambda s, zh, y, zl: (s - 1, zh, y, zl))
    incoming = send(handed_on[0, 0], lambda s, zh, y, zl: (s + 1, zh, y, zl))
    upstream, slot = after([upstream, slot], [attended])
    picked = lax.dynamic_index_in_dim(evicted[0], slot[0, 0], 0, keepdims=False)[0]
    blocks = call(columns_kernel, [wide] * 4, place, upstream, weight)
    picked, incoming, *rest = after([picked.transpose(1, 0, 2), incoming, *replicas, *blocks])
    replicas, blocks = rest[:4], rest[4:]

    def term(d, cuts=1):
        kernel = functools.partial(term_kernel, d=d, cuts=cuts)
        return call(kernel, [(8 * rows // cuts, columns)] * cuts, place, *replicas, weight)

    top, bottom, *blocks = after([*term(2, 2), *blocks])
    from_below, from_above = send(top, up), send(bottom, down)
    lines = [blocks[0]] + [
        send(blocks[j], lambda s, zh, y, zl, j=j: (s, zh, y, zl + j)) for j in range(1, 4)
    ]
    above, below = term(1)[0], term(3)[0]
    above, below, from_below, from_above, *lines = after(
        [above, below, from_below, from_above, *lines]
    )

    tall = (2 * half, columns)
    above, below, line0 = call(
        second_kernel,
        [tall, tall, (half, columns)],
        place,
        above,
        below,
        from_below,
        from_above,
        *lines,
    )
    above, below, line0, *blocks = after([above, below, line0, *blocks])
    from_below, from_above = send(above, up), send(below, down)
    lines = [
        send(blocks[j], lambda s, zh, y, zl, j=j: (s, zh ^ 1, y, zl + j)) for j in range(4)
    ]
    own = term(0)[0]
    line = call(stack_kernel, [tall], place, line0, *lines)[0]
    own, from_below, from_above = after([own, from_below, from_above])

    kept, given = call(third_kernel, [(half, columns)] * 2, place, own, from_below, from_above)
    left, right = send(line, up), send(line, down)
    given = send(given, lambda s, zh, y, zl: (s, zh ^ 1, y, zl))

    def d_term(*pieces):
        return call(gradient_kernel, [(8 * rows, group_width)], place, *pieces, weight)[0]

    fetched = send(picked, lambda s, zh, y, zl: (7 - s, zh, y, zl) if s >= 4 else None)
    near0 = d_term(line)
    terms = call(pair_kernel, [wide] * 4, place, kept, given)
    left, right, near0, fetched = after([left, right, near0, fetched])

    top, bottom = call(halves_kernel, [(half, columns)] * 2, place, left, right)
    across = [send(top, up), send(bottom, down)]
    stored = call(
        stored_kernel,
        [
            (heads, length, width3),
            jax.ShapeDtypeStruct((heads, length, length), F32),
            (heads, length, group_width // heads),
        ],
        place,
        fetched,
        fresh_heads,
    )
    terms = [terms[0]] + [
        send(terms[j], lambda s, zh, y, zl, j=j: (s, zh, y, zl - j)) for j in range(1, 4)
    ]
    near1, near3 = d_term(left), d_term(right)
    near1, near3, *rest = after([near1, near3, *across, *terms], stored)
    across, terms = rest[:2], rest[2:]

    near2 = dot(jnp.concatenate(across), weight, NT).astype(BF16)
    d_rel = jnp.stack([near0, near1, near2, near3]).reshape(4, 2, 4, rows, group_width)
    d_terms = [d_rel[:, :, 0]] + [
        send(d_rel[:, :, j], lambda s, zh, y, zl, j=j: (s, zh, y, zl - j)) for j in range(1, 4)
    ]
    layer_out = call(output_kernel, [(rows, model)], place, incoming, *terms)[0]
    grads = call(
        backward_kernel,
        [(heads, length, width3)],
        place,
        *stored,
        *d_terms,
        scratch=[(4, *block)],
    )[0]
    return (layer_out[None, None], grads.transpose(1, 0, 2)[None, None])


def solution(mesh):
    return jax.shard_map(
        shards,
        mesh=mesh,
        in_specs=(
            P("section", "dp", "tensor", None),
            P("section", "dp", "tensor", None),
            P("section", "dp", None, "tensor", None),
            P("section", None, "dp", None, "tensor", None),
            P("section", "dp"),
            P("section", "tensor", "dp"),
        ),
        out_specs=(P("section", "dp", "tensor", None), P("section", "dp", None, "tensor", None)),
        check_vma=False,
    )
```

```python
import functools
import math

import jax
import jax.numpy as jnp
from jax import lax
from jax.experimental import pallas as pl
from jax.experimental.pallas import tpu as pltpu
from jax.sharding import PartitionSpec as P

AXES = ("section", "tensor", "dp")
BF16 = jnp.bfloat16
F32 = jnp.float32
VMEM_LIMIT = 20 * 2**20


def send(block, target):
    route = []
    for s in range(8):
        for zh in range(2):
            for y in range(4):
                for zl in range(4):
                    to = target(s, zh, y, zl)
                    if to is not None:
                        s2, zh2, y2, zl2 = to
                        there = (s2 % 8 * 8 + zh2 % 2 * 4 + y2 % 4) * 4 + zl2 % 4
                        route.append((((s * 2 + zh) * 4 + y) * 4 + zl, there))
    return lax.ppermute(block, AXES, route)


def call(kernel, out_shapes, place, *arrays, scratch=()):
    return pl.pallas_call(
        kernel,
        out_shape=[
            shape if isinstance(shape, jax.ShapeDtypeStruct) else jax.ShapeDtypeStruct(shape, BF16)
            for shape in out_shapes
        ],
        in_specs=[pl.BlockSpec(memory_space=pltpu.SMEM)]
        + [pl.BlockSpec(memory_space=pltpu.VMEM)] * len(arrays),
        out_specs=[pl.BlockSpec(memory_space=pltpu.VMEM)] * len(out_shapes),
        scratch_shapes=[pltpu.VMEM(shape, BF16) for shape in scratch],
        compiler_params=pltpu.CompilerParams(vmem_limit_bytes=VMEM_LIMIT),
        cost_estimate=pl.CostEstimate(flops=0, bytes_accessed=0, transcendentals=0),
    )(place, *arrays)


def dot(a, b, contract):
    return lax.dot_general(a, b, (contract, ((), ())), preferred_element_type=F32)


NN = ((1,), (0,))
NT = ((1,), (1,))
TN = ((0,), (0,))


def probabilities(queries, key_rows):
    length, head_dim = queries.shape
    scores = dot(queries, key_rows, NT) * (1.0 / math.sqrt(head_dim))
    causal = lax.broadcasted_iota(jnp.int32, (length, length), 0) >= lax.broadcasted_iota(
        jnp.int32, (length, length), 1
    )
    scores = jnp.where(causal, scores, -1e30)
    weights = jnp.exp(scores - jnp.max(scores, axis=-1, keepdims=True))
    return weights * (1.0 / jnp.sum(weights, axis=-1, keepdims=True))


def forward_kernel(place, packed, out):
    zh, y = place[1], place[2]
    heads, length, width = packed.shape
    hd = width // 3
    rows = length // 8
    for h in range(heads):
        probs = probabilities(packed[h, :, :hd], packed[h, :, hd : 2 * hd])
        attended = dot(probs.astype(BF16), packed[h, :, 2 * hd :], NN).astype(BF16)
        for b in range(2):
            for c in range(4):
                at = (b * 4 + c) * rows
                out[(c - y) & 3, b ^ zh, :, h * hd : (h + 1) * hd] = attended[at : at + rows]


def stored_kernel(place, fetched, fresh, stored, probs, attended):
    section = place[0]
    heads, length, width = fetched.shape
    hd = width // 3
    for h in range(heads):
        packed = jnp.where(section < 4, fetched[h], fresh[h])
        stored[h] = packed
        probs[h] = probabilities(packed[:, :hd], packed[:, hd : 2 * hd])
        attended[h] = dot(probs[h].astype(BF16), packed[:, 2 * hd :], NN).astype(BF16)


def backward_kernel(place, stored, probs, attended, *refs):
    zh, y = place[1], place[2]
    terms, out, scratch = refs[:4], refs[4], refs[5]
    heads, length, width = stored.shape
    hd = width // 3
    scaling = 1.0 / math.sqrt(hd)
    scratch[...] = sum(ref[...].astype(F32) for ref in terms).astype(BF16)
    for h in range(heads):
        queries = stored[h, :, :hd]
        key_rows = stored[h, :, hd : 2 * hd]
        value_rows = stored[h, :, 2 * hd :]
        d_attended = jnp.concatenate(
            [
                scratch[(y - c) & 3, b ^ zh, :, h * hd : (h + 1) * hd]
                for b in range(2)
                for c in range(4)
            ],
            axis=0,
        )
        probs_low = probs[h].astype(BF16)
        delta = jnp.sum(
            d_attended.astype(F32) * attended[h].astype(F32), axis=-1, keepdims=True
        )
        d_values = dot(probs_low, d_attended, TN).astype(BF16)
        d_probs = dot(d_attended, value_rows, NT)
        d_scores = (probs[h] * (d_probs - delta)).astype(BF16)
        out[h, :, :hd] = (dot(d_scores, key_rows, NN) * scaling).astype(BF16)
        out[h, :, hd : 2 * hd] = (dot(d_scores, queries, TN) * scaling).astype(BF16)
        out[h, :, 2 * hd :] = d_values


def term_kernel(place, *refs, d, cuts):
    pieces, weight, outs = refs[:4], refs[4], refs[5:]
    left = jnp.concatenate([piece[d, a] for a in range(2) for piece in pieces])
    width = 512
    rows = left.shape[0] // cuts
    for at in range(0, weight.shape[1], width):
        product = dot(left, weight[:, at : at + width], NN).astype(BF16)
        for i, out in enumerate(outs):
            out[:, at : at + width] = product[i * rows : (i + 1) * rows]


def gradient_kernel(place, *refs):
    pieces, weight, out = refs[:-2], refs[-2], refs[-1]
    width = 256
    for at in range(0, out.shape[1], width):
        row = 0
        for piece in pieces:
            rows = piece.shape[0]
            out[row : row + rows, at : at + width] = dot(
                piece[...], weight[at : at + width], NT
            ).astype(BF16)
            row += rows


def columns_kernel(place, gradient, weight, *outs):
    zl = place[3]
    width = outs[0].shape[1]
    for j, out in enumerate(outs):
        out[...] = gradient[:, pl.ds(pl.multiple_of((zl ^ j) * width, width), width)]


def second_kernel(place, above, below, from_below, from_above, *refs):
    lines, (out_above, out_below, line) = refs[:4], refs[4:]
    half = from_below.shape[0]
    top, bottom = slice(0, half), slice(half, 2 * half)
    out_above[top] = (above[top].astype(F32) + from_below[...].astype(F32)).astype(BF16)
    out_above[bottom] = above[bottom]
    out_below[top] = below[top]
    out_below[bottom] = (below[bottom].astype(F32) + from_above[...].astype(F32)).astype(BF16)
    rows = lines[0].shape[0]
    for i, ref in enumerate(lines):
        line[i * rows : (i + 1) * rows] = ref[...]


def stack_kernel(place, *refs):
    out = refs[-1]
    at = 0
    for ref in refs[:-1]:
        rows = ref.shape[0]
        out[at : at + rows] = ref[...]
        at += rows


def third_kernel(place, own, left, right, *outs):
    rows = outs[0].shape[0]
    for i, out in enumerate(outs):
        at = slice(i * rows, (i + 1) * rows)
        out[...] = (
            own[at].astype(F32) + left[at].astype(F32) + right[at].astype(F32)
        ).astype(BF16)


def pair_kernel(place, one, other, *outs):
    rows = outs[0].shape[0]
    for i, out in enumerate(outs):
        at = slice(i * rows, (i + 1) * rows)
        out[...] = (one[at].astype(F32) + other[at].astype(F32)).astype(BF16)


def halves_kernel(place, left, right, top, bottom):
    half = top.shape[0]
    top[...] = left[:half]
    bottom[...] = right[half:]


def output_kernel(place, incoming, *refs):
    zl = place[3]
    terms, out = refs[:4], refs[4]
    width = terms[0].shape[1]
    for j, term in enumerate(terms):
        at = pl.ds(pl.multiple_of((zl ^ j) * width, width), width)
        out[:, at] = (incoming[:, at].astype(F32) + term[...].astype(F32)).astype(BF16)


def after(values, *others):
    flat = [leaf for other in others for leaf in other]
    return lax.optimization_barrier((*values, *flat))[: len(values)]


def shards(handed_on, handed_back, fresh, evicted, plan, w_out):
    section = lax.axis_index("section")
    tensor = lax.axis_index("tensor")
    zl = lax.axis_index("dp")
    zh, y = tensor >> 2, tensor & 3
    place = jnp.stack([section, zh, y, zl]).astype(jnp.int32)
    length, heads, width3 = fresh.shape[2:]
    rows, model = handed_on.shape[2:]
    weight = w_out[0]
    group_width, columns = weight.shape
    fresh_heads = fresh[0, 0].transpose(1, 0, 2)
    wide = (rows, columns)
    block = (2, rows, group_width)
    half = 4 * rows
    up = lambda s, zh, y, zl: (s, zh, y + 1, zl)
    down = lambda s, zh, y, zl: (s, zh, y - 1, zl)

    slot = send(plan, lambda s, zh, y, zl: (7 - s, zh, y, zl))
    attended = call(forward_kernel, [(4, *block)], place, fresh_heads)[0]
    replicas = [attended] + [
        send(attended, lambda s, zh, y, zl, j=j: (s, zh, y, zl ^ j)) for j in range(1, 4)
    ]
    upstream = send(handed_back[0, 0], lambda s, zh, y, zl: (s - 1, zh, y, zl))
    incoming = send(handed_on[0, 0], lambda s, zh, y, zl: (s + 1, zh, y, zl))
    upstream, slot = after([upstream, slot], [attended])
    picked = lax.dynamic_index_in_dim(evicted[0], slot[0, 0], 0, keepdims=False)[0]
    blocks = call(columns_kernel, [wide] * 4, place, upstream, weight)
    picked, incoming, *rest = after([picked.transpose(1, 0, 2), incoming, *replicas, *blocks])
    replicas, blocks = rest[:4], rest[4:]

    def term(d, cuts=1):
        kernel = functools.partial(term_kernel, d=d, cuts=cuts)
        return call(kernel, [(8 * rows // cuts, columns)] * cuts, place, *replicas, weight)

    top, bottom, *blocks = after([*term(2, 2), *blocks])
    from_below, from_above = send(top, up), send(bottom, down)
    lines = [blocks[0]] + [
        send(blocks[j], lambda s, zh, y, zl, j=j: (s, zh, y, zl ^ j)) for j in range(1, 4)
    ]
    above, below = term(1)[0], term(3)[0]
    above, below, from_below, from_above, *lines = after(
        [above, below, from_below, from_above, *lines]
    )

    tall = (2 * half, columns)
    above, below, line0 = call(
        second_kernel,
        [tall, tall, (half, columns)],
        place,
        above,
        below,
        from_below,
        from_above,
        *lines,
    )
    above, below, line0, *blocks = after([above, below, line0, *blocks])
    from_below, from_above = send(above, up), send(below, down)
    lines = [
        send(blocks[j], lambda s, zh, y, zl, j=j: (s, zh ^ 1, y, zl ^ j)) for j in range(4)
    ]
    own = term(0)[0]
    line = call(stack_kernel, [tall], place, line0, *lines)[0]
    own, from_below, from_above = after([own, from_below, from_above])

    kept, given = call(third_kernel, [(half, columns)] * 2, place, own, from_below, from_above)
    left, right = send(line, up), send(line, down)
    given = send(given, lambda s, zh, y, zl: (s, zh ^ 1, y, zl))

    def d_term(*pieces):
        return call(gradient_kernel, [(8 * rows, group_width)], place, *pieces, weight)[0]

    fetched = send(picked, lambda s, zh, y, zl: (7 - s, zh, y, zl) if s >= 4 else None)
    near0 = d_term(line)
    terms = call(pair_kernel, [wide] * 4, place, kept, given)
    left, right, near0, fetched = after([left, right, near0, fetched])

    top, bottom = call(halves_kernel, [(half, columns)] * 2, place, left, right)
    across = [send(top, up), send(bottom, down)]
    stored = call(
        stored_kernel,
        [
            (heads, length, width3),
            jax.ShapeDtypeStruct((heads, length, length), F32),
            (heads, length, group_width // heads),
        ],
        place,
        fetched,
        fresh_heads,
    )
    terms = [terms[0]] + [
        send(terms[j], lambda s, zh, y, zl, j=j: (s, zh, y, zl ^ j)) for j in range(1, 4)
    ]
    near1, near3 = d_term(left), d_term(right)
    near1, near3, *rest = after([near1, near3, *across, *terms], stored)
    across, terms = rest[:2], rest[2:]

    near2 = dot(jnp.concatenate(across), weight, NT).astype(BF16)
    d_rel = jnp.stack([near0, near1, near2, near3]).reshape(4, 2, 4, rows, group_width)
    d_terms = [d_rel[:, :, 0]] + [
        send(d_rel[:, :, j], lambda s, zh, y, zl, j=j: (s, zh, y, zl ^ j)) for j in range(1, 4)
    ]
    layer_out = call(output_kernel, [(rows, model)], place, incoming, *terms)[0]
    grads = call(
        backward_kernel,
        [(heads, length, width3)],
        place,
        *stored,
        *d_terms,
        scratch=[(4, *block)],
    )[0]
    return (layer_out[None, None], grads.transpose(1, 0, 2)[None, None])


def solution(mesh):
    return jax.shard_map(
        shards,
        mesh=mesh,
        in_specs=(
            P("section", "dp", "tensor", None),
            P("section", "dp", "tensor", None),
            P("section", "dp", None, "tensor", None),
            P("section", None, "dp", None, "tensor", None),
            P("section", "dp"),
            P("section", "tensor", "dp"),
        ),
        out_specs=(P("section", "dp", "tensor", None), P("section", "dp", None, "tensor", None)),
        check_vma=False,
    )
```

```python
import functools
import math

import jax
import jax.numpy as jnp
from jax import lax
from jax.experimental import pallas as pl
from jax.experimental.pallas import tpu as pltpu
from jax.sharding import PartitionSpec as P

AXES = ("section", "tensor", "dp")
BF16 = jnp.bfloat16
F32 = jnp.float32
VMEM_LIMIT = 20 * 2**20


def send(block, target):
    route = []
    for s in range(8):
        for zh in range(2):
            for y in range(4):
                for zl in range(4):
                    to = target(s, zh, y, zl)
                    if to is not None:
                        s2, zh2, y2, zl2 = to
                        there = (s2 % 8 * 8 + zh2 % 2 * 4 + y2 % 4) * 4 + zl2 % 4
                        route.append((((s * 2 + zh) * 4 + y) * 4 + zl, there))
    return lax.ppermute(block, AXES, route)


def call(kernel, out_shapes, place, *arrays, scratch=()):
    return pl.pallas_call(
        kernel,
        out_shape=[
            shape if isinstance(shape, jax.ShapeDtypeStruct) else jax.ShapeDtypeStruct(shape, BF16)
            for shape in out_shapes
        ],
        in_specs=[pl.BlockSpec(memory_space=pltpu.SMEM)]
        + [pl.BlockSpec(memory_space=pltpu.VMEM)] * len(arrays),
        out_specs=[pl.BlockSpec(memory_space=pltpu.VMEM)] * len(out_shapes),
        scratch_shapes=[pltpu.VMEM(shape, BF16) for shape in scratch],
        compiler_params=pltpu.CompilerParams(vmem_limit_bytes=VMEM_LIMIT),
        cost_estimate=pl.CostEstimate(flops=0, bytes_accessed=0, transcendentals=0),
    )(place, *arrays)


def dot(a, b, contract):
    return lax.dot_general(a, b, (contract, ((), ())), preferred_element_type=F32)


NN = ((1,), (0,))
NT = ((1,), (1,))
TN = ((0,), (0,))


def probabilities(queries, key_rows):
    length, head_dim = queries.shape
    scores = dot(queries, key_rows, NT) * (1.0 / math.sqrt(head_dim))
    causal = lax.broadcasted_iota(jnp.int32, (length, length), 0) >= lax.broadcasted_iota(
        jnp.int32, (length, length), 1
    )
    scores = jnp.where(causal, scores, -1e30)
    weights = jnp.exp(scores - jnp.max(scores, axis=-1, keepdims=True))
    return weights * (1.0 / jnp.sum(weights, axis=-1, keepdims=True))


def forward_kernel(place, packed, out):
    zh, y = place[1], place[2]
    heads, length, width = packed.shape
    hd = width // 3
    rows = length // 8
    for h in range(heads):
        probs = probabilities(packed[h, :, :hd], packed[h, :, hd : 2 * hd])
        attended = dot(probs.astype(BF16), packed[h, :, 2 * hd :], NN).astype(BF16)
        for b in range(2):
            for c in range(4):
                at = (b * 4 + c) * rows
                out[(c - y) & 3, b ^ zh, :, h * hd : (h + 1) * hd] = attended[at : at + rows]


def stored_kernel(place, fetched, fresh, stored, probs, attended):
    section = place[0]
    heads, length, width = fetched.shape
    hd = width // 3
    for h in range(heads):
        packed = jnp.where(section < 4, fetched[h], fresh[h])
        stored[h] = packed
        probs[h] = probabilities(packed[:, :hd], packed[:, hd : 2 * hd])
        attended[h] = dot(probs[h].astype(BF16), packed[:, 2 * hd :], NN).astype(BF16)


def backward_kernel(place, stored, probs, attended, *refs):
    zh, y = place[1], place[2]
    terms, out, scratch = refs[:4], refs[4], refs[5]
    heads, length, width = stored.shape
    hd = width // 3
    scaling = 1.0 / math.sqrt(hd)
    scratch[...] = sum(ref[...].astype(F32) for ref in terms).astype(BF16)
    for h in range(heads):
        queries = stored[h, :, :hd]
        key_rows = stored[h, :, hd : 2 * hd]
        value_rows = stored[h, :, 2 * hd :]
        d_attended = jnp.concatenate(
            [
                scratch[(y - c) & 3, b ^ zh, :, h * hd : (h + 1) * hd]
                for b in range(2)
                for c in range(4)
            ],
            axis=0,
        )
        probs_low = probs[h].astype(BF16)
        delta = jnp.sum(
            d_attended.astype(F32) * attended[h].astype(F32), axis=-1, keepdims=True
        )
        d_values = dot(probs_low, d_attended, TN).astype(BF16)
        d_probs = dot(d_attended, value_rows, NT)
        d_scores = (probs[h] * (d_probs - delta)).astype(BF16)
        out[h, :, :hd] = (dot(d_scores, key_rows, NN) * scaling).astype(BF16)
        out[h, :, hd : 2 * hd] = (dot(d_scores, queries, TN) * scaling).astype(BF16)
        out[h, :, 2 * hd :] = d_values


def term_kernel(place, *refs, d, cuts):
    pieces, weight, outs = refs[:4], refs[4], refs[5:]
    left = jnp.concatenate([piece[d, a] for a in range(2) for piece in pieces])
    width = 512
    rows = left.shape[0] // cuts
    for at in range(0, weight.shape[1], width):
        product = dot(left, weight[:, at : at + width], NN).astype(BF16)
        for i, out in enumerate(outs):
            out[:, at : at + width] = product[i * rows : (i + 1) * rows]


def gradient_kernel(place, *refs):
    pieces, weight, out = refs[:-2], refs[-2], refs[-1]
    width = 256
    for at in range(0, out.shape[1], width):
        row = 0
        for piece in pieces:
            rows = piece.shape[0]
            out[row : row + rows, at : at + width] = dot(
                piece[...], weight[at : at + width], NT
            ).astype(BF16)
            row += rows


def columns_kernel(place, gradient, weight, *outs):
    zl = place[3]
    width = outs[0].shape[1]
    for j, out in enumerate(outs):
        out[...] = gradient[:, pl.ds(pl.multiple_of(((zl + j) & 3) * width, width), width)]


def second_kernel(place, above, below, from_below, from_above, *refs):
    lines, (out_above, out_below, line) = refs[:4], refs[4:]
    half = from_below.shape[0]
    top, bottom = slice(0, half), slice(half, 2 * half)
    out_above[top] = (above[top].astype(F32) + from_below[...].astype(F32)).astype(BF16)
    out_above[bottom] = above[bottom]
    out_below[top] = below[top]
    out_below[bottom] = (below[bottom].astype(F32) + from_above[...].astype(F32)).astype(BF16)
    rows = lines[0].shape[0]
    for i, ref in enumerate(lines):
        line[i * rows : (i + 1) * rows] = ref[...]


def stack_kernel(place, *refs):
    out = refs[-1]
    at = 0
    for ref in refs[:-1]:
        rows = ref.shape[0]
        out[at : at + rows] = ref[...]
        at += rows


def third_kernel(place, own, left, right, *outs):
    rows = outs[0].shape[0]
    for i, out in enumerate(outs):
        at = slice(i * rows, (i + 1) * rows)
        out[...] = (
            own[at].astype(F32) + left[at].astype(F32) + right[at].astype(F32)
        ).astype(BF16)


def pair_kernel(place, one, other, *outs):
    rows = outs[0].shape[0]
    for i, out in enumerate(outs):
        at = slice(i * rows, (i + 1) * rows)
        out[...] = (one[at].astype(F32) + other[at].astype(F32)).astype(BF16)


def halves_kernel(place, left, right, top, bottom):
    half = top.shape[0]
    top[...] = left[:half]
    bottom[...] = right[half:]


def output_kernel(place, incoming, *refs):
    zl = place[3]
    terms, out = refs[:4], refs[4]
    width = terms[0].shape[1]
    for j, term in enumerate(terms):
        at = pl.ds(pl.multiple_of(((zl + j) & 3) * width, width), width)
        out[:, at] = (incoming[:, at].astype(F32) + term[...].astype(F32)).astype(BF16)


def after(values, *others):
    flat = [leaf for other in others for leaf in other]
    return lax.optimization_barrier((*values, *flat))[: len(values)]


def shards(handed_on, handed_back, fresh, evicted, plan, w_out):
    section = lax.axis_index("section")
    tensor = lax.axis_index("tensor")
    zl = lax.axis_index("dp")
    zh, y = tensor >> 2, tensor & 3
    place = jnp.stack([section, zh, y, zl]).astype(jnp.int32)
    length, heads, width3 = fresh.shape[2:]
    rows, model = handed_on.shape[2:]
    weight = w_out[0]
    group_width, columns = weight.shape
    fresh_heads = fresh[0, 0].transpose(1, 0, 2)
    wide = (rows, columns)
    block = (2, rows, group_width)
    half = 4 * rows
    up = lambda s, zh, y, zl: (s, zh, y + 1, zl)
    down = lambda s, zh, y, zl: (s, zh, y - 1, zl)

    slot = send(plan, lambda s, zh, y, zl: (7 - s, zh, y, zl))
    attended = call(forward_kernel, [(4, *block)], place, fresh_heads)[0]
    replicas = [attended] + [
        send(attended, lambda s, zh, y, zl, j=j: (s, zh, y, zl + j)) for j in range(1, 4)
    ]
    upstream = send(handed_back[0, 0], lambda s, zh, y, zl: (s - 1, zh, y, zl))
    incoming = send(handed_on[0, 0], lambda s, zh, y, zl: (s + 1, zh, y, zl))
    upstream, slot = after([upstream, slot], [attended])
    picked = lax.dynamic_index_in_dim(evicted[0], slot[0, 0], 0, keepdims=False)[0]
    blocks = call(columns_kernel, [wide] * 4, place, upstream, weight)
    picked, incoming, *rest = after([picked.transpose(1, 0, 2), incoming, *replicas, *blocks])
    replicas, blocks = rest[:4], rest[4:]

    def term(d, cuts=1):
        kernel = functools.partial(term_kernel, d=d, cuts=cuts)
        return call(kernel, [(8 * rows // cuts, columns)] * cuts, place, *replicas, weight)

    top, bottom, *blocks = after([*term(2, 2), *blocks])
    from_below, from_above = send(top, up), send(bottom, down)
    lines = [blocks[0]] + [
        send(blocks[j], lambda s, zh, y, zl, j=j: (s, zh, y, zl + j)) for j in range(1, 4)
    ]
    above, below = term(1)[0], term(3)[0]
    above, below, from_below, from_above, *lines = after(
        [above, below, from_below, from_above, *lines]
    )

    tall = (2 * half, columns)
    above, below, line0 = call(
        second_kernel,
        [tall, tall, (half, columns)],
        place,
        above,
        below,
        from_below,
        from_above,
        *lines,
    )
    above, below, line0, *blocks = after([above, below, line0, *blocks])
    from_below, from_above = send(above, up), send(below, down)
    lines = [
        send(blocks[j], lambda s, zh, y, zl, j=j: (s, zh ^ 1, y, zl + j)) for j in range(4)
    ]
    own = term(0)[0]
    line = call(stack_kernel, [tall], place, line0, *lines)[0]
    own, from_below, from_above = after([own, from_below, from_above])

    kept, given = call(third_kernel, [(half, columns)] * 2, place, own, from_below, from_above)
    left, right = send(line, up), send(line, down)
    given = send(given, lambda s, zh, y, zl: (s, zh ^ 1, y, zl))

    def d_term(*pieces):
        return call(gradient_kernel, [(8 * rows, group_width)], place, *pieces, weight)[0]

    fetched = send(picked, lambda s, zh, y, zl: (7 - s, zh, y, zl) if s >= 4 else None)
    near0 = d_term(line)
    terms = call(pair_kernel, [wide] * 4, place, kept, given)
    left, right, near0, fetched = after([left, right, near0, fetched])

    top, bottom = call(halves_kernel, [(half, columns)] * 2, place, left, right)
    across = [send(top, up), send(bottom, down)]
    stored = call(
        stored_kernel,
        [
            (heads, length, width3),
            jax.ShapeDtypeStruct((heads, length, length), F32),
            (heads, length, group_width // heads),
        ],
        place,
        fetched,
        fresh_heads,
    )
    terms = [terms[0]] + [
        send(terms[j], lambda s, zh, y, zl, j=j: (s, zh, y, zl - j)) for j in range(1, 4)
    ]
    near1, near3 = d_term(left), d_term(right)
    near1, near3, *rest = after([near1, near3, *across, *terms])
    across, terms = rest[:2], rest[2:]

    near2 = dot(jnp.concatenate(across), weight, NT).astype(BF16)
    d_rel = jnp.stack([near0, near1, near2, near3]).reshape(4, 2, 4, rows, group_width)
    d_terms = [d_rel[:, :, 0]] + [
        send(d_rel[:, :, j], lambda s, zh, y, zl, j=j: (s, zh, y, zl - j)) for j in range(1, 4)
    ]
    layer_out = call(output_kernel, [(rows, model)], place, incoming, *terms)[0]
    grads = call(
        backward_kernel,
        [(heads, length, width3)],
        place,
        *stored,
        *d_terms,
        scratch=[(4, *block)],
    )[0]
    return (layer_out[None, None], grads.transpose(1, 0, 2)[None, None])


def solution(mesh):
    return jax.shard_map(
        shards,
        mesh=mesh,
        in_specs=(
            P("section", "dp", "tensor", None),
            P("section", "dp", "tensor", None),
            P("section", "dp", None, "tensor", None),
            P("section", None, "dp", None, "tensor", None),
            P("section", "dp"),
            P("section", "tensor", "dp"),
        ),
        out_specs=(P("section", "dp", "tensor", None), P("section", "dp", None, "tensor", None)),
        check_vma=False,
    )
```
